128 devices in a mesh: context: 32 (over x_lo, y, z), tensor: 4 (over x_hi, core).
Axes of the slice: x: 4 (x_hi: 2, x_lo: 2; x = x_hi * 2 + x_lo), y: 4, z: 4, core: 2. Of those that a mesh axis runs over, the one named last changes fastest.
Arguments:
- query: bfloat16 [4096, 4096], P('context', 'tensor'), may hold values from -6 to 6
- key_feat: bfloat16 [4096, 4096], P('context', 'tensor'), may hold values from -6 to 6
- value_feat: bfloat16 [4096, 4096], P('context', 'tensor'), may hold values from -6 to 6
- filt: bfloat16 [4096, 4096], P('context', 'tensor'), may hold values from -1 to 1
- skip: float32 [4096], P('tensor'), may hold values from 0.5 to 1.5
- dout: bfloat16 [4096, 4096], P('context', 'tensor'), may hold values from -6 to 6
- w_out: bfloat16 [4096, 4096], P('tensor', 'context'), may hold values from -0.09375 to 0.09375
Outputs:
- grad_query: bfloat16 [4096, 4096], P('context', 'tensor')
- grad_key: bfloat16 [4096, 4096], P('context', 'tensor')
- grad_value: bfloat16 [4096, 4096], P('context', 'tensor')
- grad_filt: bfloat16 [4096, 4096], P('context', 'tensor')
- wo_grad: float32 [4096, 4096], P('tensor', 'context')
The draws below stay inside these ranges and needn't reach their ends.
All inputs are finite; a program needn't handle non-finite values.
Results may differ from the reference program's by a relative error of at most 0.0058.
Values may be sent and summed in bfloat16 or wider, within the bound.
No kernel may reach another device: no remote copies, remote signals or barrier semaphores. Data moves between devices by JAX's collectives and lax.ppermute only.
A program may use at most 128 MiB of HBM per device.

```python
import math
import jax
import jax.numpy as jnp
from jax import lax

C = 4096
TOKENS = 4096


def draw_filt(key, part):
    key = jax.random.fold_in(key, 11)
    rate_key, noise_key = jax.random.split(key)
    log_rate = jax.random.uniform(rate_key, (C,), jnp.float32, math.log(0.1 / TOKENS), math.log(1.0 / 30.0))
    noise = 1.0 + 0.6 * jnp.clip(jax.random.normal(noise_key, (TOKENS, C), jnp.float32), -4.0, 4.0)
    rate = jnp.exp(log_rate)
    amplitude = jnp.sqrt(2.0 * rate / (1.0 - jnp.exp(-2.0 * rate * TOKENS)))
    lags = jnp.arange(TOKENS, dtype=jnp.float32)[:, None]
    return (amplitude * jnp.exp(-rate * lags) * noise).astype(jnp.bfloat16)


def raised(values, stream_key, source, target, shards_of, factor):
    owner, partner = [(jnp.arange(values.shape[dim]) // (values.shape[dim] // shards_of)).reshape([-1 if axis == dim else 1 for axis in range(values.ndim)]) for dim in (source, target)]
    chosen = jax.random.permutation(stream_key, shards_of)[partner]
    strong = (owner == chosen) | (owner == (partner + shards_of // 2) % shards_of)
    return jnp.where(strong, factor * values, values)


def block_scale(rng, dims, pieces, least, high):
    def one(dim, blocks):
        steps = jax.random.uniform(jax.random.fold_in(jax.random.fold_in(rng, 6), dim), (blocks,), jnp.float32, least / len(pieces), high / len(pieces))
        return jnp.repeat(jnp.exp(steps), dims[dim] // blocks).reshape((-1,) + (1,) * (len(dims) - dim - 1))

    factor_of = one(*pieces[0])
    for cut in pieces[1:]:
        factor_of = factor_of * one(*cut)
    return factor_of


def bell_draw(key, extent, width, limit, cuts=(), kind=jnp.bfloat16):
    values = width * jax.random.normal(key, extent, jnp.float32)
    if cuts:
        values = values * block_scale(key, extent, cuts, -0.22, 0.18)
    return jnp.clip(values, -limit, limit).astype(kind)


def heavy_noise(rng, shape, scale, bound, cuts, heavy, held_as=jnp.bfloat16):
    drawn = scale * jax.random.normal(rng, shape, jnp.float32)
    if cuts:
        drawn = drawn * block_scale(rng, shape, cuts, -0.22, 0.18)
    return jnp.clip(raised(drawn, jax.random.fold_in(rng, 3), *heavy), -bound, bound).astype(held_as)


def setup_inputs(seed: int = 0) -> dict:
    key_list = jax.random.split(jax.random.key(seed), 8)
    return {
        "query": bell_draw(key_list[0], (TOKENS, C), 1.0, 6.0, ((0, 32), (1, 4))),
        "key_feat": bell_draw(key_list[1], (TOKENS, C), 1.0, 6.0, ((0, 32), (1, 4))),
        "value_feat": bell_draw(key_list[2], (TOKENS, C), 1.0, 6.0, ((0, 32), (1, 4))),
        "filt": draw_filt(jax.random.fold_in(key_list[7], 71), 0),
        "skip": jnp.clip(0.5 + 1.0 * jax.random.uniform(key_list[4], (C,), jnp.float32) ** block_scale(key_list[4], (C,), ((0, 4),), -0.2, 0.2), 0.5, 1.5),
        "dout": heavy_noise(key_list[5], (TOKENS, C), 1.0, 6.0, ((0, 32), (1, 4)), (0, 1, 32, 2.75)),
        "w_out": bell_draw(key_list[6], (C, C), C ** -0.5, 0.09375, ((0, 4), (1, 32))),
    }


def channel_block(blocks):
    signal_b, filt_b, grad_b, skip_b = blocks
    length = signal_b.shape[1]
    total = 2 * length
    signal_s = jnp.fft.rfft(signal_b, n=total, axis=1)
    filt_s = jnp.fft.rfft(filt_b, n=total, axis=1)
    grad_s = jnp.fft.rfft(grad_b, n=total, axis=1)
    conv = jnp.fft.irfft(filt_s * signal_s, n=total, axis=1)[:, :length] + skip_b[:, None] * signal_b
    back = jnp.fft.irfft(jnp.conj(filt_s) * grad_s, n=total, axis=1)[:, :length] + skip_b[:, None] * grad_b
    lagged = jnp.fft.irfft(jnp.conj(signal_s) * grad_s, n=total, axis=1)[:, :length]
    return conv.astype(jnp.bfloat16), back.astype(jnp.bfloat16), lagged.astype(jnp.bfloat16)


def reference(query, key_feat, value_feat, filt, skip, dout, w_out):
    grady = jnp.dot(dout, w_out.T, preferred_element_type=jnp.float32)
    grad_gate = (grady * query.astype(jnp.float32)).astype(jnp.bfloat16)
    signal = (key_feat.astype(jnp.float32) * value_feat.astype(jnp.float32)).astype(jnp.bfloat16)
    block = math.gcd(C, 256)
    nblock = C // block

    def split_channels(array):
        return array.astype(jnp.float32).T.reshape(nblock, block, TOKENS)

    conv, back, lagged = lax.map(channel_block, (split_channels(signal), split_channels(filt), split_channels(grad_gate), skip.astype(jnp.float32).reshape(nblock, block)))

    def join_channels(array):
        return array.reshape(C, TOKENS).T

    conv_out = join_channels(conv).astype(jnp.float32)
    grad_signal = join_channels(back).astype(jnp.float32)
    grad_filt = join_channels(lagged)
    gated = (query.astype(jnp.float32) * conv_out).astype(jnp.bfloat16)
    grad_query = (grady * conv_out).astype(jnp.bfloat16)
    grad_key = (grad_signal * value_feat.astype(jnp.float32)).astype(jnp.bfloat16)
    grad_value = (grad_signal * key_feat.astype(jnp.float32)).astype(jnp.bfloat16)
    wo_grad = jnp.dot(gated.T, dout, preferred_element_type=jnp.float32)
    return grad_query, grad_key, grad_value, grad_filt, wo_grad
```

```python
import functools

import jax
import jax.numpy as jnp
import numpy as np
from jax import lax
from jax.experimental import pallas as pl
from jax.experimental.pallas import tpu as pltpu
from jax.sharding import Mesh
from jax.sharding import PartitionSpec as P

BF16 = jnp.bfloat16
F32 = jnp.float32
VMEM = pl.BlockSpec(memory_space=pltpu.VMEM)
SMEM = pl.BlockSpec(memory_space=pltpu.SMEM)
PARAMS = pltpu.CompilerParams(vmem_limit_bytes=48 * 1024 * 1024)

M, N = 32, 128
GROUP = 8


def split(values):
    high = values.astype(jnp.bfloat16)
    return high, (values - high.astype(values.dtype)).astype(jnp.bfloat16)


@functools.cache
def tables():
    k1, m, n = np.arange(M) + 0.25, np.arange(M), np.arange(N)
    first = 2 * np.pi * np.outer(k1, m) / M
    second = 2 * np.pi * np.outer(n, n) / N
    turn = 2 * np.pi * np.outer(k1, n) / (M * N)
    eye = np.eye(GROUP)
    one = np.kron(np.concatenate([np.cos(first), -np.sin(first)]), eye)
    cos, sin = np.cos(second), np.sin(second)
    two = np.block([[cos, -sin], [sin, cos]])
    back_two = np.block([[cos, sin], [-sin, cos]])
    back_one = one.T / (M * N)

    def pair(table):
        high = table.astype(jnp.bfloat16)
        low = (table - high.astype(np.float64)).astype(jnp.bfloat16)
        return high, low

    spread = [np.repeat(f(turn), GROUP, axis=0).astype(np.float32) for f in (np.cos, np.sin)]
    return (*pair(one), *pair(two), *pair(back_two), *pair(back_one), *spread)


def dot(lhs, rhs):
    return jnp.dot(lhs, rhs, preferred_element_type=F32)


def rows_of(block, group):
    part = block[:, group * GROUP : (group + 1) * GROUP, :]
    return part.reshape(M * GROUP, N).astype(BF16)


def forward(sides, tabs):
    one_h, one_l, two_h, two_l = (t[...] for t in tabs[:4])
    cos, sin = tabs[8][...], tabs[9][...]
    cat = jnp.concatenate(sides, axis=1)
    part = dot(one_h, cat) + dot(one_l, cat)
    half = part.shape[0] // 2
    out = []
    for index in range(len(sides)):
        lanes = slice(index * N, (index + 1) * N)
        re, im = part[:half, lanes], part[half:, lanes]
        turned = jnp.concatenate([re * cos + im * sin, im * cos - re * sin], axis=1)
        high, low = split(turned)
        out.append(dot(high, two_h) + dot(low, two_h) + dot(high, two_l))
    return out


def inverse(specs, tabs):
    two_h, two_l, one_h, one_l = (t[...] for t in tabs[4:8])
    cos, sin = tabs[8][...], tabs[9][...]
    cols = []
    for spec in specs:
        high, low = split(spec)
        part = dot(high, two_h) + dot(low, two_h) + dot(high, two_l)
        re, im = part[:, :N], part[:, N:]
        cols.append(jnp.concatenate([re * cos - im * sin, im * cos + re * sin], axis=0))
    high, low = split(jnp.concatenate(cols, axis=1))
    full = dot(one_h, high) + dot(one_h, low) + dot(one_l, high)
    return [full[:, i * N : (i + 1) * N] for i in range(len(specs))]


def times(a, b, conj_a):
    are, aim, bre, bim = a[:, :N], a[:, N:], b[:, :N], b[:, N:]
    if conj_a:
        return jnp.concatenate([are * bre + aim * bim, are * bim - aim * bre], axis=1)
    return jnp.concatenate([are * bre - aim * bim, are * bim + aim * bre], axis=1)


def pair_of(first, second):
    shape = (M, GROUP, N)
    return jnp.concatenate([first.reshape(shape), second.reshape(shape)], axis=1)


def prep_kernel(key_ref, value_ref, filt_ref, query_ref, out_ref):
    def put(which, block):
        out_ref[:, which] = block.T.reshape(M, 32, N).astype(BF16)

    signal = key_ref[...].astype(F32) * value_ref[...].astype(F32)
    put(0, signal.astype(BF16).astype(F32))
    put(1, filt_ref[...].astype(F32))
    put(2, query_ref[...].astype(F32))


def conv_kernel(in_ref, skip_ref, *refs):
    tabs, (conv_ref, gated_ref, sig_ref, fil_ref) = refs[:10], refs[10:]
    signal, filt, query = (in_ref[:, i].astype(F32) for i in range(3))
    for pair in range(2):
        groups = (2 * pair, 2 * pair + 1)
        chans = slice(16 * pair, 16 * pair + 16)
        spectra = forward([rows_of(a, g) for a in (signal, filt) for g in groups], tabs)
        for i, g in enumerate(groups):
            sig_ref[g], fil_ref[g] = spectra[i], spectra[2 + i]
        conv = pair_of(*inverse([times(spectra[i], spectra[2 + i], False) for i in range(2)], tabs))
        conv = conv + skip_ref[chans, :][None] * signal[:, chans, :]
        conv = conv.astype(BF16)
        conv_ref[:, chans, :] = conv
        gated = (query[:, chans, :] * conv.astype(F32)).astype(BF16)
        for xl in range(2):
            for y in range(4):
                block = gated[xl * 16 + y * 4 : xl * 16 + y * 4 + 4]
                for copy in range(4):
                    gated_ref[y, copy, xl * 4 : xl * 4 + 4, chans, :] = block


def back_kernel(part_ref, in_ref, conv_ref, skip_ref, sig_ref, fil_ref, *refs):
    tabs, out_ref, gate_s = refs[:10], refs[10], refs[11]
    for y in range(4):
        for b in range(8):
            total = part_ref[4 * y, b].astype(F32)
            for z in range(1, 4):
                total = total + part_ref[4 * y + z, b].astype(F32)
            m = (b // 4) * 16 + y * 4 + b % 4
            out_ref[m, 0] = (total * conv_ref[m].astype(F32)).astype(BF16)
            gate_s[m] = (total * in_ref[m, 2].astype(F32)).astype(BF16).astype(F32)
    gate = gate_s[...]
    for pair in range(2):
        groups = (2 * pair, 2 * pair + 1)
        chans = slice(16 * pair, 16 * pair + 16)
        spectra = forward([rows_of(gate, g) for g in groups], tabs)
        specs = [times(fil_ref[g], s, True) for g, s in zip(groups, spectra)]
        specs += [times(sig_ref[g], s, True) for g, s in zip(groups, spectra)]
        result = inverse(specs, tabs)
        back = pair_of(*result[:2]) + skip_ref[chans, :][None] * gate[:, chans, :]
        out_ref[:, 1, chans, :] = back.astype(BF16)
        out_ref[:, 2, chans, :] = pair_of(*result[2:]).astype(BF16)


def final_kernel(in_ref, key_ref, value_ref, gq_ref, gk_ref, gv_ref, gf_ref):
    def get(which):
        return in_ref[:, which].astype(F32).reshape(M * 32, N).T

    gq_ref[...] = get(0).astype(BF16)
    gf_ref[...] = get(2).astype(BF16)
    back = get(1)
    gk_ref[...] = (back * value_ref[...].astype(F32)).astype(BF16)
    gv_ref[...] = (back * key_ref[...].astype(F32)).astype(BF16)


def grady_kernel(where_ref, *refs):
    d_refs, w_refs, (out_ref, d_ref), w_s = refs[:8], refs[8:12], refs[12:14], refs[14]
    xl, y, q = where_ref[0], where_ref[1], where_ref[2]
    for p in range(8):
        for lo in range(2):
            d_ref[xl ^ (p & 1), 2 * (q ^ (p >> 1)) + lo] = d_refs[p][:, lo]
    for s in range(4):
        for i in range(2):
            w_s[(xl ^ i) * 4 + (y ^ s)] = w_refs[s][i]
    lhs = jnp.concatenate([w_s[j] for j in range(8)], axis=1)
    for side in range(2):
        for z in range(0, 4, 2):
            rhs = jnp.concatenate(
                [d_ref[side, j, z : z + 2].reshape(2 * N, 128) for j in range(8)], axis=1
            )
            part = lax.dot_general(lhs, rhs, (((1,), (1,)), ((), ())), preferred_element_type=F32)
            part = part.astype(BF16)
            for k in range(2):
                out_ref[:, side * 4 + z + k] = part[:, k * N : (k + 1) * N].reshape(16, 32, N)


def wo_kernel(gated_ref, d_ref, out_ref):
    lhs = jnp.concatenate([gated_ref[:, b].reshape(512, N) for b in range(8)], axis=1)
    for j in range(0, 8, 2):
        rhs = jnp.concatenate(
            [
                jnp.concatenate([d_ref[xl, j + k].reshape(512, 128) for xl in range(2)], axis=0)
                for k in range(2)
            ],
            axis=1,
        )
        part = dot(lhs, rhs).astype(BF16)
        for k in range(2):
            out_ref[j + k] = part[:, k * 128 : (k + 1) * 128]


def sum_kernel(in_ref, out_ref):
    for xl in range(2):
        total = in_ref[4 * xl].astype(F32)
        for y in range(1, 4):
            total = total + in_ref[4 * xl + y].astype(F32)
        out_ref[xl * 512 : xl * 512 + 512, :] = total


def call(kernel, ins, outs, scratch=(), first=VMEM):
    return pl.pallas_call(
        kernel,
        out_shape=outs,
        in_specs=[first] + [VMEM] * (len(ins) - 1),
        out_specs=jax.tree.map(lambda _: VMEM, outs),
        scratch_shapes=list(scratch),
        compiler_params=PARAMS,
    )(*ins)


def shape(*dims, dtype=BF16):
    return jax.ShapeDtypeStruct(dims, dtype)


CONTEXT = ("xl", "y", "z")


def flip(value, axes, sizes, by):
    total = int(np.prod(sizes))
    return lax.ppermute(value, axes, [(i, i ^ by) for i in range(total)])


def exchange(value, axes):
    return lax.all_to_all(value, axes, 0, 0)


def body(query, key_feat, value_feat, filt, skip, dout, w_out):
    xl, y, z = (lax.axis_index(a) for a in CONTEXT)
    q = lax.axis_index("xh") * 2 + lax.axis_index("co")
    tabs = tables()
    skip_c = lax.dynamic_slice_in_dim(skip, (xl * 16 + y * 4 + z) * 32, 32, 0)
    skip_c = jnp.broadcast_to(skip_c[:, None], (32, N))

    with jax.named_scope("gather_d"):
        d = dout.reshape(128, 2, 4, 128).transpose(2, 1, 0, 3)
        d = exchange(d, "z")
        d = [d] + [flip(d, ("xl", "xh"), (2, 2), (p & 1) * 2 + (p >> 1)) for p in (1, 2, 3)]
        d_pieces = {}
        for p in range(4):
            a, b = p & 1, p >> 1
            d_pieces[a + 2 * (2 * b)] = d[p]
            d_pieces[a + 2 * (2 * b + 1)] = flip(d[p], "co", (2,), 1)
        d_pieces = [d_pieces[p] for p in range(8)]
    with jax.named_scope("gather_w"):
        halves = w_out.reshape(2, 512, 128)
        keep = lax.dynamic_index_in_dim(halves, xl, 0, keepdims=False)
        give = lax.dynamic_index_in_dim(halves, 1 - xl, 0, keepdims=False)
        w = jnp.stack([keep, flip(give, "xl", (2,), 1)])
        w_pieces = [w] + [flip(w, "y", (4,), s) for s in (1, 2, 3)]

    with jax.named_scope("to_channels"):
        sent = call(prep_kernel, (key_feat, value_feat, filt, query), shape(M, 3, 32, N))
        held = exchange(sent, CONTEXT)
    with jax.named_scope("conv"):
        conv, gated, sig, fil = call(
            conv_kernel,
            (held, skip_c, *tabs),
            (
                shape(M, 32, N),
                shape(4, 4, 8, 32, N),
                shape(4, 256, 256, dtype=F32),
                shape(4, 256, 256, dtype=F32),
            ),
        )
    with jax.named_scope("grady"):
        part, d_all = call(
            grady_kernel,
            (jnp.stack([xl, y, q]).astype(jnp.int32), *d_pieces, *w_pieces),
            (shape(16, 8, 32, N), shape(2, 8, 4, 128, 128)),
            [pltpu.VMEM((8, 512, 128), BF16)],
            SMEM,
        )
        part = exchange(part, ("y", "z"))
    with jax.named_scope("gated"):
        gated = exchange(gated.reshape(16, 8, 32, N), ("y", "z"))
    with jax.named_scope("back"):
        sent = call(
            back_kernel,
            (part, held, conv, skip_c, sig, fil, *tabs),
            shape(M, 3, 32, N),
            [pltpu.VMEM((M, 32, N), F32)],
        )
        got = exchange(sent, CONTEXT)
    with jax.named_scope("wo"):
        wo = call(wo_kernel, (gated, d_all), shape(8, 512, 128))
        wo = exchange(wo, ("xl", "y"))
        wo_grad = call(sum_kernel, (wo,), shape(1024, 128, dtype=F32))
    with jax.named_scope("final"):
        grads = call(final_kernel, (got, key_feat, value_feat), [shape(128, 1024)] * 4)
    return (*grads, wo_grad)


def solution(mesh):
    fine = Mesh(mesh.devices.reshape(2, 4, 4, 2, 2), ("xl", "y", "z", "xh", "co"))
    tokens, channels = P(CONTEXT, ("xh", "co")), P(("xh", "co"))
    rows = P(("xh", "co"), CONTEXT)
    return jax.shard_map(
        body,
        mesh=fine,
        in_specs=(tokens, tokens, tokens, tokens, channels, tokens, rows),
        out_specs=(tokens, tokens, tokens, tokens, rows),
        check_vma=False,
    )
```

```python
import functools

import jax
import jax.numpy as jnp
import numpy as np
from jax import lax
from jax.experimental import pallas as pl
from jax.experimental.pallas import tpu as pltpu
from jax.sharding import Mesh
from jax.sharding import PartitionSpec as P

BF16 = jnp.bfloat16
F32 = jnp.float32
HBM = pl.BlockSpec(memory_space=pltpu.HBM)
PARAMS = pltpu.CompilerParams(vmem_limit_bytes=63 * 1024 * 1024)

M, N = 32, 128
GROUP = 8


def split(values):
    high = values.astype(jnp.bfloat16)
    return high, (values - high.astype(values.dtype)).astype(jnp.bfloat16)


@functools.cache
def tables():
    k1, m, n = np.arange(M) + 0.25, np.arange(M), np.arange(N)
    first = 2 * np.pi * np.outer(k1, m) / M
    second = 2 * np.pi * np.outer(n, n) / N
    turn = 2 * np.pi * np.outer(k1, n) / (M * N)
    eye = np.eye(GROUP)
    one = np.kron(np.concatenate([np.cos(first), -np.sin(first)]), eye)
    cos, sin = np.cos(second), np.sin(second)
    two = np.block([[cos, -sin], [sin, cos]])
    back_two = np.block([[cos, sin], [-sin, cos]])
    back_one = one.T / (M * N)

    parts = []
    for table in (one, two, back_two, back_one[:, :256], back_one[:, 256:]):
        high = table.astype(jnp.bfloat16)
        parts += [high, (table - high.astype(np.float64)).astype(jnp.bfloat16)]
    return np.concatenate(parts), np.stack([np.cos(turn), np.sin(turn)]).astype(np.float32)


ROWS = {}
for _name, _count in (("one", 512), ("two", 256), ("back_two", 256), ("left", 256), ("right", 256)):
    for _part in "hl":
        ROWS[_name, _part] = (sum(n for _, n in ROWS.values()), _count)


def table(tabs, name):
    return [tabs[0][start : start + count] for start, count in (ROWS[name, p] for p in "hl")]


def turns(tabs):
    return [
        jnp.broadcast_to(tabs[1][i][:, None, :], (M, GROUP, N)).reshape(M * GROUP, N)
        for i in range(2)
    ]


def dot(lhs, rhs):
    return jnp.dot(lhs, rhs, preferred_element_type=F32)


def rows_of(block, group):
    part = block[:, group * GROUP : (group + 1) * GROUP, :]
    return part.reshape(M * GROUP, N).astype(BF16)


def forward(sides, tabs):
    (one_h, one_l), (two_h, two_l) = table(tabs, "one"), table(tabs, "two")
    cos, sin = turns(tabs)
    cat = jnp.concatenate(sides, axis=1)
    part = dot(one_h, cat) + dot(one_l, cat)
    half = part.shape[0] // 2
    out = []
    for index in range(len(sides)):
        lanes = slice(index * N, (index + 1) * N)
        re, im = part[:half, lanes], part[half:, lanes]
        turned = jnp.concatenate([re * cos + im * sin, im * cos - re * sin], axis=1)
        high, low = split(turned)
        out.append(dot(high, two_h) + dot(low, two_h) + dot(high, two_l))
    return out


def inverse(specs, tabs):
    two_h, two_l = table(tabs, "back_two")
    one_h, one_l = (jnp.concatenate(p, axis=1) for p in zip(table(tabs, "left"), table(tabs, "right")))
    cos, sin = turns(tabs)
    cols = []
    for spec in specs:
        high, low = split(spec)
        part = dot(high, two_h) + dot(low, two_h) + dot(high, two_l)
        re, im = part[:, :N], part[:, N:]
        cols.append(jnp.concatenate([re * cos - im * sin, im * cos + re * sin], axis=0))
    high, low = split(jnp.concatenate(cols, axis=1))
    full = dot(one_h, high) + dot(one_h, low) + dot(one_l, high)
    return [full[:, i * N : (i + 1) * N] for i in range(len(specs))]


def times(a, b, conj_a):
    are, aim, bre, bim = a[:, :N], a[:, N:], b[:, :N], b[:, N:]
    if conj_a:
        return jnp.concatenate([are * bre + aim * bim, are * bim - aim * bre], axis=1)
    return jnp.concatenate([are * bre - aim * bim, are * bim + aim * bre], axis=1)


def pair_of(first, second):
    shape = (M, GROUP, N)
    return jnp.concatenate([first.reshape(shape), second.reshape(shape)], axis=1)


def prep_kernel(where, ins, outs, scratch, ready, emit):
    key_ref, value_ref, filt_ref, query_ref, skip_ref, w_ref, d_ref = ins
    (skip_s,) = scratch
    xl, y, z = where[0], where[1], where[3]

    def put(which, block):
        outs[0][:, which] = block.T.reshape(M, 32, N).astype(BF16)
        emit(0, slice(None), which)

    ready(0, 1)
    signal = key_ref[...].astype(F32) * value_ref[...].astype(F32)
    put(0, signal.astype(BF16).astype(F32))
    ready(2)
    put(1, filt_ref[...].astype(F32))
    ready(3)
    put(2, query_ref[...].astype(F32))
    ready(6)
    for to_y in range(4):
        for to_z in range(4):
            for lo in range(2):
                first = (4 * lo + to_z) * 128
                block = d_ref[32 * to_y : 32 * to_y + 32, first : first + 128]
                for side in range(2):
                    outs[0][side * 16 + to_y * 4 + to_z, 3 + lo] = block
    emit(0, slice(None), slice(3, 5))
    ready(4)
    row = jnp.broadcast_to(skip_ref[pl.ds(xl * 4 + y, 1), :], (N, N))
    skip_s[...] = row.T.reshape(4, 32, N)
    outs[3][...] = skip_s[z]
    emit(3)
    ready(5)
    for i in range(2):
        outs[1 + i][...] = w_ref[xl ^ i]
        emit(1 + i)


def swap_quarters(blocks):
    quarter = lax.broadcasted_iota(jnp.int32, blocks[0].shape, blocks[0].ndim - 1) // 32
    axis = blocks[0].ndim - 1
    out = []
    for r in range(4):
        total = blocks[r]
        for y in range(4):
            if y != r:
                total = jnp.where(
                    quarter == y, pltpu.roll(blocks[y], (y - r) * 32 % N, axis), total
                )
        out.append(total)
    return out


def conv_kernel(_, ins, outs, scratch, ready, emit):
    in_ref, skip_ref, *tabs = ins
    conv_ref, gated_ref, sig_ref, fil_ref = outs
    ready(0)
    signal, filt, query = (in_ref[:, i].astype(F32) for i in range(3))
    ready(1, 2, 3)
    for pair in range(2):
        groups = (2 * pair, 2 * pair + 1)
        chans = slice(16 * pair, 16 * pair + 16)
        spectra = forward([rows_of(a, g) for a in (signal, filt) for g in groups], tabs)
        for i, g in enumerate(groups):
            sig_ref[g], fil_ref[g] = spectra[i], spectra[2 + i]
        emit(2, slice(2 * pair, 2 * pair + 2))
        emit(3, slice(2 * pair, 2 * pair + 2))
        conv = pair_of(*inverse([times(spectra[i], spectra[2 + i], False) for i in range(2)], tabs))
        conv = conv + skip_ref[chans, :][None] * signal[:, chans, :]
        conv = conv.astype(BF16)
        conv_ref[:, chans, :] = conv
        gated = (query[:, chans, :] * conv.astype(F32)).reshape(8, 4, 16, N)
        for y, block in enumerate(swap_quarters([gated[:, r] for r in range(4)])):
            for copy in range(4):
                gated_ref[y, copy, :, chans, :] = block.astype(BF16)
        every = slice(None)
        emit(1, every, every, every, chans)
        emit(0, every, chans)


def back_kernel(_, ins, outs, scratch, ready, emit):
    part_ref, in_ref, conv_ref, skip_ref, sig_ref, fil_ref, *tabs = ins
    (out_ref,), (gate_s,) = outs, scratch
    ready(0, 1, 2)
    for g in range(8):
        totals = []
        for y in range(4):
            total = part_ref[4 * y, g].astype(F32)
            for z in range(1, 4):
                total = total + part_ref[4 * y + z, g].astype(F32)
            totals.append(total)
        for r, grady in enumerate(swap_quarters(totals)):
            m = 4 * g + r
            out_ref[m, 0] = (grady * conv_ref[m].astype(F32)).astype(BF16)
            gate_s[m] = (grady * in_ref[m].astype(F32)).astype(BF16).astype(F32)
    emit(0, slice(None), 0)
    gate = gate_s[...]
    ready(*range(3, 8))
    for pair in range(2):
        groups = (2 * pair, 2 * pair + 1)
        chans = slice(16 * pair, 16 * pair + 16)
        spectra = forward([rows_of(gate, g) for g in groups], tabs)
        specs = [times(fil_ref[g], s, True) for g, s in zip(groups, spectra)]
        specs += [times(sig_ref[g], s, True) for g, s in zip(groups, spectra)]
        result = inverse(specs, tabs)
        back = pair_of(*result[:2]) + skip_ref[chans, :][None] * gate[:, chans, :]
        out_ref[:, 1, chans, :] = back.astype(BF16)
        emit(0, slice(None), 1, chans)
        out_ref[:, 2, chans, :] = pair_of(*result[2:]).astype(BF16)
        emit(0, slice(None), 2, chans)


def final_kernel(_, ins, outs, scratch, ready, emit):
    in_ref, key_ref, value_ref = ins

    def get(which):
        return in_ref[:, which].astype(F32).reshape(M * 32, N).T

    def put(which, block):
        outs[which][...] = block.astype(BF16)
        emit(which)

    ready(0)
    put(0, get(0))
    put(3, get(2))
    ready(1, 2)
    back = get(1)
    put(1, back * value_ref[...].astype(F32))
    put(2, back * key_ref[...].astype(F32))


def grady_kernel(where, ins, outs, scratch, ready, emit):
    d_refs, w_refs, (out_ref, d_ref), (w_s,) = ins[:4], ins[4:], outs, scratch
    xl, y, q = where[0], where[1], where[2]
    for p in range(4):
        ready(p)
        for lo in range(2):
            d_ref[2 * (q ^ (2 * (p & 1) + (p >> 1))) + lo] = d_refs[p][:, lo]
    emit(1)
    for s in range(4):
        ready(4 + s)
        for i in range(2):
            w_s[(xl ^ i) * 4 + (y ^ s)] = w_refs[s][i]
    lhs = jnp.concatenate([w_s[j] for j in range(8)], axis=1)
    for g in range(0, 8, 2):
        rhs = jnp.concatenate(
            [d_ref[j, 4 * g : 4 * g + 8].reshape(2 * N, 128) for j in range(8)], axis=1
        )
        part = lax.dot_general(lhs, rhs, (((1,), (1,)), ((), ())), preferred_element_type=F32)
        part = part.astype(BF16)
        for k in range(2):
            out_ref[:, g + k] = part[:, k * N : (k + 1) * N].reshape(16, 32, N)
        emit(0, slice(None), slice(g, g + 2))


def wo_kernel(where, ins, outs, scratch, ready, emit):
    (gated_ref, d_ref), (all_s,) = ins, scratch
    ready(0, 1)
    lhs = jnp.concatenate([gated_ref[:, b].reshape(512, N) for b in range(8)], axis=1)
    for xl in range(2):
        for to in range(0, 4, 2):
            rhs = jnp.concatenate(
                [d_ref[xl * 4 + to + k].reshape(1024, 128) for k in range(2)], axis=1
            )
            part = dot(lhs, rhs)
            for k in range(2):
                all_s[to + k, xl] = part[:, k * 128 : (k + 1) * 128].astype(BF16)
    for s in range(4):
        outs[s][...] = all_s[where[1] ^ s]
        emit(s)


def give_kernel(where, ins, outs, scratch, ready, emit):
    ready(0, 1, 2, 3)
    total = ins[0][where[0] ^ 1].astype(F32)
    for s in range(1, 4):
        total = total + ins[s][where[0] ^ 1].astype(F32)
    outs[0][...] = total.astype(BF16)
    emit(0)


def join_kernel(where, ins, outs, scratch, ready, emit):
    ready(0, 1, 2, 3, 4)
    total = ins[0][where[0]].astype(F32)
    for s in range(1, 4):
        total = total + ins[s][where[0]].astype(F32)
    outs[0][where[0]] = total
    outs[0][where[0] ^ 1] = ins[4][...].astype(F32)
    emit(0)


def call(kernel, ins, outs, scratch=(), parts={}, cost=2):
    n_in, n_out = len(ins), len(outs)

    def whole(*refs):
        xl, y, z, xh, co = (lax.axis_index(a) for a in ("xl", "y", "z", "xh", "co"))
        where = (xl, y, 2 * xh + co, z)
        hbm_in, refs = refs[:n_in], refs[n_in:]
        hbm_out, refs = refs[:n_out], refs[n_out:]
        in_refs, refs = refs[:n_in], refs[n_in:]
        out_refs, refs = refs[:n_out], refs[n_out:]
        (in_sem, out_sem), rest = refs[:2], refs[2:]
        loads = [
            pltpu.make_async_copy(
                hbm_in[i].at[parts[i]] if i in parts else hbm_in[i], in_refs[i], in_sem.at[i]
            )
            for i in range(n_in)
        ]
        for load in loads:
            load.start()
        waited, stores = set(), []

        def ready(*which):
            for i in which:
                if i not in waited:
                    waited.add(i)
                    loads[i].wait()

        def emit(j, *index):
            source, target = out_refs[j], hbm_out[j]
            if index:
                source, target = source.at[index], target.at[index]
            stores.append(pltpu.make_async_copy(source, target, out_sem.at[len(stores)]))
            stores[-1].start()

        kernel(where, in_refs, out_refs, rest, ready, emit)
        ready(*range(n_in))
        for store in stores:
            store.wait()

    shapes = [
        jax.eval_shape(lambda x, i=i: x[parts[i]], a) if i in parts else a
        for i, a in enumerate(ins)
    ]
    buffers = [pltpu.VMEM(a.shape, a.dtype) for a in (*shapes, *outs)]
    return pl.pallas_call(
        whole,
        out_shape=list(outs),
        in_specs=[HBM] * n_in,
        out_specs=[HBM] * n_out,
        scratch_shapes=buffers
        + [pltpu.SemaphoreType.DMA((n_in,)), pltpu.SemaphoreType.DMA((16,))]
        + list(scratch),
        compiler_params=PARAMS,
        cost_estimate=pl.CostEstimate(
            flops=0, bytes_accessed=cost * 3_000_000, transcendentals=0
        ),
    )(*ins)


def shape(*dims, dtype=BF16):
    return jax.ShapeDtypeStruct(dims, dtype)


CONTEXT = ("xl", "y", "z")


def flip(value, axes, sizes, by):
    total = int(np.prod(sizes))
    return lax.ppermute(value, axes, [(i, i ^ by) for i in range(total)])


def exchange(value, axes):
    return lax.all_to_all(value, axes, 0, 0)


def body(query, key_feat, value_feat, filt, skip, dout, w_out):
    tabs = tables()

    with jax.named_scope("prepare"):
        sent, keep, give, skip_c = call(
            prep_kernel,
            (key_feat, value_feat, filt, query, skip.reshape(8, 128), w_out.reshape(2, 512, 128), dout),
            [shape(M, 5, 32, N)] + [shape(512, 128)] * 2 + [shape(32, N, dtype=F32)],
            [pltpu.VMEM((4, 32, N), F32)],
            cost=3,
        )
    with jax.named_scope("to_channels"):
        held = exchange(sent, CONTEXT)
    with jax.named_scope("gather_w"):
        take = flip(give, "xl", (2,), 1)
    held, take = lax.optimization_barrier((held, take))
    with jax.named_scope("gather_d"):
        d = held[:, 3:]
        d = [d, flip(d, ("xl", "xh"), (2, 2), 3)]
    with jax.named_scope("gather_w"):
        w = jnp.stack([keep, take])
        w = [w] + [flip(w, "y", (4,), s) for s in (1, 2, 3)]
    with jax.named_scope("conv"):
        conv, gated, sig, fil = call(
            conv_kernel,
            (held, skip_c, *tabs),
            (
                shape(M, 32, N),
                shape(4, 4, 8, 32, N),
                shape(4, 256, 256, dtype=F32),
                shape(4, 256, 256, dtype=F32),
            ),
            (),
            {0: (slice(None), slice(0, 3))},
            cost=20,
        )
    gated, d, w = lax.optimization_barrier((gated, d, w))
    with jax.named_scope("gated"):
        gated = exchange(gated.reshape(16, 8, 32, N), ("y", "z"))
    with jax.named_scope("gather_d"):
        d_pieces = d + [flip(piece, "co", (2,), 1) for piece in d]
    with jax.named_scope("grady"):
        part, d_all = call(
            grady_kernel,
            (*d_pieces, *w),
            (shape(16, 8, 32, N), shape(8, 32, 32, 128)),
            [pltpu.VMEM((8, 512, 128), BF16)],
            cost=5,
        )
        part, gated = lax.optimization_barrier((part, gated))
        part = exchange(part, ("y", "z"))
    with jax.named_scope("wo"):
        wo = call(
            wo_kernel,
            (gated, d_all),
            [shape(2, 512, 128)] * 4,
            [pltpu.VMEM((4, 2, 512, 128), BF16)],
            cost=5,
        )
        part, _ = lax.optimization_barrier((part, wo))
        wo = [wo[0]] + [flip(wo[s], "y", (4,), s) for s in (1, 2, 3)]
    with jax.named_scope("back"):
        (sent,) = call(
            back_kernel,
            (part, held, conv, skip_c, sig, fil, *tabs),
            [shape(M, 3, 32, N)],
            [pltpu.VMEM((M, 32, N), F32)],
            {1: (slice(None), 2)},
            cost=7,
        )
    with jax.named_scope("wo"):
        sent, wo = lax.optimization_barrier((sent, wo))
        (give,) = call(give_kernel, wo, [shape(512, 128)])
        sent, give = lax.optimization_barrier((sent, give))
        take = flip(give, "xl", (2,), 1)
    with jax.named_scope("back"):
        got = exchange(sent, CONTEXT)
    with jax.named_scope("wo"):
        (wo_grad,) = call(
            join_kernel, (*wo, take), [shape(2, 512, 128, dtype=F32)]
        )
    with jax.named_scope("final"):
        grads = call(final_kernel, (got, key_feat, value_feat), [shape(128, 1024)] * 4)
    return (*grads, wo_grad.reshape(1024, 128))


def solution(mesh):
    fine = Mesh(mesh.devices.reshape(2, 4, 4, 2, 2), ("xl", "y", "z", "xh", "co"))
    tokens, channels = P(CONTEXT, ("xh", "co")), P(("xh", "co"))
    rows = P(("xh", "co"), CONTEXT)
    return jax.shard_map(
        body,
        mesh=fine,
        in_specs=(tokens, tokens, tokens, tokens, channels, tokens, rows),
        out_specs=(tokens, tokens, tokens, tokens, rows),
        check_vma=False,
    )
```

```python
import functools

import jax
import jax.numpy as jnp
import numpy as np
from jax import lax
from jax.experimental import pallas as pl
from jax.experimental.pallas import tpu as pltpu
from jax.sharding import Mesh
from jax.sharding import PartitionSpec as P

BF16 = jnp.bfloat16
F32 = jnp.float32
PARAMS = pltpu.CompilerParams(vmem_limit_bytes=16 * 1024 * 1024)

M, N = 32, 128
GROUP = 8


def split(values):
    high = values.astype(jnp.bfloat16)
    return high, (values - high.astype(values.dtype)).astype(jnp.bfloat16)


@functools.cache
def tables():
    k1, m, n = np.arange(M) + 0.25, np.arange(M), np.arange(N)
    first = 2 * np.pi * np.outer(k1, m) / M
    second = 2 * np.pi * np.outer(n, n) / N
    turn = 2 * np.pi * np.outer(k1, n) / (M * N)
    eye = np.eye(GROUP)
    one = np.kron(np.concatenate([np.cos(first), -np.sin(first)]), eye)
    cos, sin = np.cos(second), np.sin(second)
    two = np.block([[cos, -sin], [sin, cos]])
    back_two = np.block([[cos, sin], [-sin, cos]])
    back_one = one.T / (M * N)

    parts = []
    for table in (one, two, back_two, back_one[:, :256], back_one[:, 256:]):
        high = table.astype(jnp.bfloat16)
        parts += [high, (table - high.astype(np.float64)).astype(jnp.bfloat16)]
    return np.concatenate(parts), np.stack([np.cos(turn), np.sin(turn)]).astype(np.float32)


ROWS = {}
for _name, _count in (("one", 512), ("two", 256), ("back_two", 256), ("left", 256), ("right", 256)):
    for _part in "hl":
        ROWS[_name, _part] = (sum(n for _, n in ROWS.values()), _count)


def table(tabs, name):
    return [tabs[0][start : start + count] for start, count in (ROWS[name, p] for p in "hl")]


def turns(tabs):
    return [
        jnp.broadcast_to(tabs[1][i][:, None, :], (M, GROUP, N)).reshape(M * GROUP, N)
        for i in range(2)
    ]


def dot(lhs, rhs):
    return jnp.dot(lhs, rhs, preferred_element_type=F32)


def rows_of(block, group):
    part = block[:, group * GROUP : (group + 1) * GROUP, :]
    return part.reshape(M * GROUP, N).astype(BF16)


def forward(sides, tabs):
    (one_h, one_l), (two_h, two_l) = table(tabs, "one"), table(tabs, "two")
    cos, sin = turns(tabs)
    cat = jnp.concatenate(sides, axis=1)
    part = dot(one_h, cat) + dot(one_l, cat)
    half = part.shape[0] // 2
    out = []
    for index in range(len(sides)):
        lanes = slice(index * N, (index + 1) * N)
        re, im = part[:half, lanes], part[half:, lanes]
        turned = jnp.concatenate([re * cos + im * sin, im * cos - re * sin], axis=1)
        high, low = split(turned)
        out.append(dot(high, two_h) + dot(low, two_h) + dot(high, two_l))
    return out


def inverse(specs, tabs):
    two_h, two_l = table(tabs, "back_two")
    one_h, one_l = (jnp.concatenate(p, axis=1) for p in zip(table(tabs, "left"), table(tabs, "right")))
    cos, sin = turns(tabs)
    cols = []
    for spec in specs:
        high, low = split(spec)
        part = dot(high, two_h) + dot(low, two_h) + dot(high, two_l)
        re, im = part[:, :N], part[:, N:]
        cols.append(jnp.concatenate([re * cos - im * sin, im * cos + re * sin], axis=0))
    high, low = split(jnp.concatenate(cols, axis=1))
    full = dot(one_h, high) + dot(one_h, low) + dot(one_l, high)
    return [full[:, i * N : (i + 1) * N] for i in range(len(specs))]


def times(a, b, conj_a):
    are, aim, bre, bim = a[:, :N], a[:, N:], b[:, :N], b[:, N:]
    if conj_a:
        return jnp.concatenate([are * bre + aim * bim, are * bim - aim * bre], axis=1)
    return jnp.concatenate([are * bre - aim * bim, are * bim + aim * bre], axis=1)


def pair_of(first, second):
    shape = (M, GROUP, N)
    return jnp.concatenate([first.reshape(shape), second.reshape(shape)], axis=1)


def prep_kernel(where, ins, outs, scratch, ready, emit):
    key_ref, value_ref, filt_ref, query_ref, skip_ref, w_ref, d_ref = ins
    (skip_s,) = scratch
    xl, y, z = where[0], where[1], where[3]

    def put(which, block):
        outs[0][:, which] = block.T.reshape(M, 32, N).astype(BF16)
        emit(0, slice(None), which)

    ready(0, 1)
    signal = key_ref[...].astype(F32) * value_ref[...].astype(F32)
    put(0, signal.astype(BF16).astype(F32))
    ready(2)
    put(1, filt_ref[...].astype(F32))
    ready(3)
    put(2, query_ref[...].astype(F32))
    ready(6)
    for to_y in range(4):
        for to_z in range(4):
            for lo in range(2):
                first = (4 * lo + to_z) * 128
                block = d_ref[32 * to_y : 32 * to_y + 32, first : first + 128]
                for side in range(2):
                    outs[0][side * 16 + to_y * 4 + to_z, 3 + lo] = block
    emit(0, slice(None), slice(3, 5))
    ready(4)
    row = jnp.broadcast_to(skip_ref[pl.ds(xl * 4 + y, 1), :], (N, N))
    skip_s[...] = row.T.reshape(4, 32, N)
    outs[3][...] = skip_s[z]
    emit(3)
    ready(5)
    for i in range(2):
        outs[1 + i][...] = w_ref[xl ^ i]
        emit(1 + i)


def swap_quarters(blocks):
    quarter = lax.broadcasted_iota(jnp.int32, blocks[0].shape, blocks[0].ndim - 1) // 32
    axis = blocks[0].ndim - 1
    out = []
    for r in range(4):
        total = blocks[r]
        for y in range(4):
            if y != r:
                total = jnp.where(
                    quarter == y, pltpu.roll(blocks[y], (y - r) * 32 % N, axis), total
                )
        out.append(total)
    return out


def conv_kernel(_, ins, outs, scratch, ready, emit):
    in_ref, skip_ref, *tabs = ins
    conv_ref, gated_ref, sig_ref, fil_ref = outs
    ready(0)
    signal, filt, query = (in_ref[:, i].astype(F32) for i in range(3))
    ready(1, 2, 3)
    for pair in range(2):
        groups = (2 * pair, 2 * pair + 1)
        chans = slice(16 * pair, 16 * pair + 16)
        spectra = forward([rows_of(a, g) for a in (signal, filt) for g in groups], tabs)
        for i, g in enumerate(groups):
            sig_ref[g], fil_ref[g] = spectra[i], spectra[2 + i]
        emit(2, slice(2 * pair, 2 * pair + 2))
        emit(3, slice(2 * pair, 2 * pair + 2))
        conv = pair_of(*inverse([times(spectra[i], spectra[2 + i], False) for i in range(2)], tabs))
        conv = conv + skip_ref[chans, :][None] * signal[:, chans, :]
        conv = conv.astype(BF16)
        conv_ref[:, chans, :] = conv
        gated = (query[:, chans, :] * conv.astype(F32)).reshape(8, 4, 16, N)
        for y, block in enumerate(swap_quarters([gated[:, r] for r in range(4)])):
            for copy in range(4):
                gated_ref[y, copy, :, chans, :] = block.astype(BF16)
        every = slice(None)
        emit(1, every, every, every, chans)
        emit(0, every, chans)


def back_kernel(_, ins, outs, scratch, ready, emit):
    part_ref, in_ref, conv_ref, skip_ref, sig_ref, fil_ref, *tabs = ins
    (out_ref,), (gate_s,) = outs, scratch
    ready(0, 1, 2)
    for g in range(8):
        totals = []
        for y in range(4):
            total = part_ref[4 * y, g].astype(F32)
            for z in range(1, 4):
                total = total + part_ref[4 * y + z, g].astype(F32)
            totals.append(total)
        for r, grady in enumerate(swap_quarters(totals)):
            m = 4 * g + r
            out_ref[m, 0] = (grady * conv_ref[m].astype(F32)).astype(BF16)
            gate_s[m] = (grady * in_ref[m].astype(F32)).astype(BF16).astype(F32)
    emit(0, slice(None), 0)
    gate = gate_s[...]
    ready(*range(3, 8))
    for pair in range(2):
        groups = (2 * pair, 2 * pair + 1)
        chans = slice(16 * pair, 16 * pair + 16)
        spectra = forward([rows_of(gate, g) for g in groups], tabs)
        specs = [times(fil_ref[g], s, True) for g, s in zip(groups, spectra)]
        specs += [times(sig_ref[g], s, True) for g, s in zip(groups, spectra)]
        result = inverse(specs, tabs)
        back = pair_of(*result[:2]) + skip_ref[chans, :][None] * gate[:, chans, :]
        out_ref[:, 1, chans, :] = back.astype(BF16)
        emit(0, slice(None), 1, chans)
        out_ref[:, 2, chans, :] = pair_of(*result[2:]).astype(BF16)
        emit(0, slice(None), 2, chans)


def final_kernel(where, ins, outs, scratch, ready, emit):
    *got, key_ref, value_ref, wo_0, wo_1, wo_2, wo_3, take_ref = ins
    wo_refs, wo_ref = (wo_0, wo_1, wo_2, wo_3), outs[4]

    def get(which):
        ready(which)
        return got[which][...].astype(F32).reshape(M * 32, N).T

    def put(which, block):
        outs[which][...] = block.astype(BF16)
        emit(which)

    put(0, get(0))
    put(3, get(1))
    back = get(2)
    ready(3, 4)
    put(1, back * value_ref[...].astype(F32))
    put(2, back * key_ref[...].astype(F32))
    ready(*range(5, 10))
    total = wo_refs[0][...].astype(F32)
    for s in range(1, 4):
        total = total + wo_refs[s][...].astype(F32)
    wo_ref[where[0]] = total
    wo_ref[where[0] ^ 1] = take_ref[...].astype(F32)
    emit(4)


def grady_kernel(where, ins, outs, scratch, ready, emit):
    d_refs, w_refs, (out_ref, d_ref), (w_s,) = ins[:4], ins[4:], outs, scratch
    xl, y, q = where[0], where[1], where[2]
    for p in range(4):
        ready(p)
        for lo in range(2):
            d_ref[2 * (q ^ (2 * (p & 1) + (p >> 1))) + lo] = d_refs[p][:, lo]
    emit(1)
    for s in range(4):
        ready(4 + s)
        for i in range(2):
            w_s[(xl ^ i) * 4 + (y ^ s)] = w_refs[s][i]
    lhs = jnp.concatenate([w_s[j] for j in range(8)], axis=1)
    for g in range(0, 8, 2):
        rhs = jnp.concatenate(
            [d_ref[j, 4 * g : 4 * g + 8].reshape(2 * N, 128) for j in range(8)], axis=1
        )
        part = lax.dot_general(lhs, rhs, (((1,), (1,)), ((), ())), preferred_element_type=F32)
        part = part.astype(BF16)
        for k in range(2):
            out_ref[:, g + k] = part[:, k * N : (k + 1) * N].reshape(16, 32, N)
        emit(0, slice(None), slice(g, g + 2))


def wo_kernel(where, ins, outs, scratch, ready, emit):
    (gated_ref, d_ref), (all_s,) = ins, scratch
    ready(0, 1)
    lhs = jnp.concatenate([gated_ref[:, b].reshape(512, N) for b in range(8)], axis=1)
    for j in range(0, 8, 2):
        rhs = jnp.concatenate([d_ref[j + k].reshape(1024, 128) for k in range(2)], axis=1)
        part = dot(lhs, rhs)
        for k in range(2):
            column = j + k
            all_s[column % 4, column // 4] = part[:, k * 128 : (k + 1) * 128].astype(BF16)
    for s in range(4):
        outs[s][...] = all_s[where[1] ^ s]
        emit(s)


def give_kernel(where, ins, outs, scratch, ready, emit):
    ready(0, 1, 2, 3)
    total = ins[0][...].astype(F32)
    for s in range(1, 4):
        total = total + ins[s][...].astype(F32)
    outs[0][...] = total.astype(BF16)
    emit(0)


def index(part, xl):
    return {"xl": xl, "other": xl ^ 1}[part] if isinstance(part, str) else part


def call(kernel, ins, outs, scratch=(), parts={}, homes="", cost=2):
    n_in, n_out = len(ins), len(outs)
    in_homes, out_homes = homes[:n_in], homes[n_in:]
    assert len(out_homes) == n_out

    def whole(*refs):
        xl, y, z, xh, co = (lax.axis_index(a) for a in ("xl", "y", "z", "xh", "co"))
        where = (xl, y, 2 * xh + co, z)
        in_homes_refs, refs = list(refs[:n_in]), refs[n_in:]
        out_homes_refs, refs = refs[:n_out], refs[n_out:]
        in_copies, refs = refs[: in_homes.count("h")], refs[in_homes.count("h") :]
        out_copies, refs = list(refs[: out_homes.count("h")]), refs[out_homes.count("h") :]
        (in_sem, out_sem), rest = refs[:2], refs[2:]
        in_refs, loads, stores = [], {}, []
        for i, ref in enumerate(in_homes_refs):
            if i in parts:
                ref = ref.at[index(parts[i], xl)]
            if in_homes[i] == "h":
                copy = in_copies[len(loads)]
                loads[i] = pltpu.make_async_copy(ref, copy, in_sem.at[len(loads)])
                loads[i].start()
                ref = copy
            in_refs.append(ref)
        out_refs = [
            out_copies.pop(0) if out_homes[j] == "h" else out_homes_refs[j] for j in range(n_out)
        ]

        def ready(*which):
            for i in which:
                if i in loads:
                    loads.pop(i).wait()

        def emit(j, *index):
            if out_homes[j] == "v":
                return
            source, target = out_refs[j], out_homes_refs[j]
            if index:
                source, target = source.at[index], target.at[index]
            stores.append(pltpu.make_async_copy(source, target, out_sem.at[len(stores)]))
            stores[-1].start()

        kernel(where, in_refs, out_refs, rest, ready, emit)
        ready(*range(n_in))
        for store in stores:
            store.wait()

    shapes = [
        jax.eval_shape(lambda x, i=i: x[index(parts[i], 0)], a) if i in parts else a
        for i, a in enumerate(ins)
    ]
    buffers = [
        pltpu.VMEM(a.shape, a.dtype) for a, home in zip((*shapes, *outs), homes) if home == "h"
    ]
    spaces = {"v": pltpu.VMEM, "h": pltpu.HBM}
    specs = [pl.BlockSpec(memory_space=spaces[home]) for home in homes]
    return pl.pallas_call(
        whole,
        out_shape=[spaces[home](a.shape, a.dtype) for a, home in zip(outs, out_homes)],
        in_specs=specs[:n_in],
        out_specs=specs[n_in:],
        scratch_shapes=buffers
        + [pltpu.SemaphoreType.DMA((max(n_in, 1),)), pltpu.SemaphoreType.DMA((16,))]
        + list(scratch),
        compiler_params=PARAMS,
        cost_estimate=pl.CostEstimate(
            flops=0, bytes_accessed=cost * 3_000_000, transcendentals=0
        ),
    )(*[pltpu.with_memory_space_constraint(a, spaces[home]) for a, home in zip(ins, in_homes)])


def shape(*dims, dtype=BF16):
    return jax.ShapeDtypeStruct(dims, dtype)


CONTEXT = ("xl", "y", "z")


def flip(value, axes, sizes, by):
    total = int(np.prod(sizes))
    return lax.ppermute(value, axes, [(i, i ^ by) for i in range(total)])


def exchange(value, axes):
    return lax.all_to_all(value, axes, 0, 0)


def body(query, key_feat, value_feat, filt, skip, dout, w_out):
    tabs = tables()

    with jax.named_scope("prepare"):
        sent, keep, give, skip_c = call(
            prep_kernel,
            (key_feat, value_feat, filt, query, skip.reshape(8, 128), w_out.reshape(2, 512, 128), dout),
            [shape(M, 5, 32, N)] + [shape(512, 128)] * 2 + [shape(32, N, dtype=F32)],
            [pltpu.VMEM((4, 32, N), F32)],
            homes="hhhhhhh" + "hvvv",
            cost=3,
        )
    with jax.named_scope("to_channels"):
        held = exchange(sent, CONTEXT)
    with jax.named_scope("gather_w"):
        take = flip(give, "xl", (2,), 1)
    held, take = lax.optimization_barrier((held, take))
    with jax.named_scope("gather_d"):
        d = held[:, 3:]
        d = [d, flip(d, ("xl", "xh"), (2, 2), 3)]
    with jax.named_scope("gather_w"):
        w = jnp.stack([keep, take])
        w = [w] + [flip(w, "y", (4,), s) for s in (1, 2, 3)]
    with jax.named_scope("conv"):
        conv, gated, sig, fil = call(
            conv_kernel,
            (held, skip_c, *tabs),
            (
                shape(M, 32, N),
                shape(4, 4, 8, 32, N),
                shape(4, 256, 256, dtype=F32),
                shape(4, 256, 256, dtype=F32),
            ),
            (),
            {0: (slice(None), slice(0, 3))},
            homes="vvvv" + "hhhh",
            cost=20,
        )
    gated, w = lax.optimization_barrier((gated, w))
    with jax.named_scope("gated"):
        gated = exchange(gated.reshape(16, 8, 32, N), ("y", "z"))
    with jax.named_scope("gather_d"):
        d_pieces = d + [flip(piece, "co", (2,), 1) for piece in d]
    with jax.named_scope("grady"):
        part, d_all = call(
            grady_kernel,
            (*d_pieces, *w),
            (shape(16, 8, 32, N), shape(8, 32, 32, 128)),
            [pltpu.VMEM((8, 512, 128), BF16)],
            homes="hvvv" + "h" * 4 + "hh",
            cost=5,
        )
        part, gated = lax.optimization_barrier((part, gated))
        part = exchange(part, ("y", "z"))
    with jax.named_scope("wo"):
        wo = call(
            wo_kernel,
            (gated, d_all),
            [shape(2, 512, 128)] * 4,
            [pltpu.VMEM((4, 2, 512, 128), BF16)],
            homes="vh" + "vvvv",
            cost=5,
        )
        part, _ = lax.optimization_barrier((part, wo))
        wo = [wo[0]] + [flip(wo[s], "y", (4,), s) for s in (1, 2, 3)]
    with jax.named_scope("back"):
        (sent,) = call(
            back_kernel,
            (part, held, conv, skip_c, sig, fil, *tabs),
            [shape(M, 3, 32, N)],
            [pltpu.VMEM((M, 32, N), F32)],
            {1: (slice(None), 2)},
            homes="hhhhhhvv" + "h",
            cost=7,
        )
    with jax.named_scope("wo"):
        sent, wo = lax.optimization_barrier((sent, wo))
        (give,) = call(
            give_kernel, wo, [shape(512, 128)], (), {i: "other" for i in range(4)}, "vvvvv"
        )
        sent, give = lax.optimization_barrier((sent, give))
        take = flip(give, "xl", (2,), 1)
    with jax.named_scope("back"):
        got = exchange(sent, CONTEXT)
    with jax.named_scope("final"):
        *grads, wo_grad = call(
            final_kernel,
            (got, got, got, key_feat, value_feat, *wo, take),
            [shape(128, 1024)] * 4 + [shape(2, 512, 128, dtype=F32)],
            (),
            {0: (slice(None), 0), 1: (slice(None), 2), 2: (slice(None), 1)}
            | {i: "xl" for i in range(5, 9)},
            "vvv" + "h" * 7 + "h" * 5,
        )
    return (*grads, wo_grad.reshape(1024, 128))


def solution(mesh):
    fine = Mesh(mesh.devices.reshape(2, 4, 4, 2, 2), ("xl", "y", "z", "xh", "co"))
    tokens, channels = P(CONTEXT, ("xh", "co")), P(("xh", "co"))
    rows = P(("xh", "co"), CONTEXT)
    return jax.shard_map(
        body,
        mesh=fine,
        in_specs=(tokens, tokens, tokens, tokens, channels, tokens, rows),
        out_specs=(tokens, tokens, tokens, tokens, rows),
        check_vma=False,
    )
```

```python
import functools

import jax
import jax.numpy as jnp
import numpy as np
from jax import lax
from jax.experimental import pallas as pl
from jax.experimental.pallas import tpu as pltpu
from jax.sharding import Mesh
from jax.sharding import PartitionSpec as P

BF16 = jnp.bfloat16
F32 = jnp.float32
PARAMS = pltpu.CompilerParams(vmem_limit_bytes=16 * 1024 * 1024)

M, N = 32, 128
GROUP = 8


def split(values):
    high = values.astype(jnp.bfloat16)
    return high, (values - high.astype(values.dtype)).astype(jnp.bfloat16)


@functools.cache
def tables():
    k1, m, n = np.arange(M) + 0.25, np.arange(M), np.arange(N)
    first = 2 * np.pi * np.outer(k1, m) / M
    second = 2 * np.pi * np.outer(n, n) / N
    turn = 2 * np.pi * np.outer(k1, n) / (M * N)
    eye = np.eye(GROUP)
    one = np.kron(np.concatenate([np.cos(first), -np.sin(first)]), eye)
    cos, sin = np.cos(second), np.sin(second)
    two = np.block([[cos, -sin], [sin, cos]])
    back_two = np.block([[cos, sin], [-sin, cos]])
    back_one = one.T / (M * N)

    parts = []
    for table in (one, two, back_two, back_one[:, :256], back_one[:, 256:]):
        high = table.astype(jnp.bfloat16)
        parts += [high, (table - high.astype(np.float64)).astype(jnp.bfloat16)]
    return np.concatenate(parts), np.stack([np.cos(turn), np.sin(turn)]).astype(np.float32)


ROWS = {}
for _name, _count in (("one", 512), ("two", 256), ("back_two", 256), ("left", 256), ("right", 256)):
    for _part in "hl":
        ROWS[_name, _part] = (sum(n for _, n in ROWS.values()), _count)


def table(tabs, name):
    return [tabs[0][start : start + count] for start, count in (ROWS[name, p] for p in "hl")]


def turns(tabs):
    return [
        jnp.broadcast_to(tabs[1][i][:, None, :], (M, GROUP, N)).reshape(M * GROUP, N)
        for i in range(2)
    ]


def dot(lhs, rhs):
    return jnp.dot(lhs, rhs, preferred_element_type=F32)


def rows_of(block, group):
    part = block[:, group * GROUP : (group + 1) * GROUP, :]
    return part.reshape(M * GROUP, N).astype(BF16)


def forward(sides, tabs):
    (one_h, one_l), (two_h, two_l) = table(tabs, "one"), table(tabs, "two")
    cos, sin = turns(tabs)
    cat = jnp.concatenate(sides, axis=1)
    part = dot(one_h, cat) + dot(one_l, cat)
    half = part.shape[0] // 2
    out = []
    for index in range(len(sides)):
        lanes = slice(index * N, (index + 1) * N)
        re, im = part[:half, lanes], part[half:, lanes]
        turned = jnp.concatenate([re * cos + im * sin, im * cos - re * sin], axis=1)
        high, low = split(turned)
        out.append(dot(high, two_h) + dot(low, two_h) + dot(high, two_l))
    return out


def inverse(specs, tabs):
    two_h, two_l = table(tabs, "back_two")
    one_h, one_l = (jnp.concatenate(p, axis=1) for p in zip(table(tabs, "left"), table(tabs, "right")))
    cos, sin = turns(tabs)
    cols = []
    for spec in specs:
        high, low = split(spec)
        part = dot(high, two_h) + dot(low, two_h) + dot(high, two_l)
        re, im = part[:, :N], part[:, N:]
        cols.append(jnp.concatenate([re * cos - im * sin, im * cos + re * sin], axis=0))
    high, low = split(jnp.concatenate(cols, axis=1))
    full = dot(one_h, high) + dot(one_h, low) + dot(one_l, high)
    return [full[:, i * N : (i + 1) * N] for i in range(len(specs))]


def times(a, b, conj_a):
    are, aim, bre, bim = a[:, :N], a[:, N:], b[:, :N], b[:, N:]
    if conj_a:
        return jnp.concatenate([are * bre + aim * bim, are * bim - aim * bre], axis=1)
    return jnp.concatenate([are * bre - aim * bim, are * bim + aim * bre], axis=1)


def pair_of(first, second):
    shape = (M, GROUP, N)
    return jnp.concatenate([first.reshape(shape), second.reshape(shape)], axis=1)


def prep_kernel(where, ins, outs, scratch, ready, emit):
    key_ref, value_ref, filt_ref, query_ref, skip_ref, w_ref, d_ref = ins
    (skip_s,) = scratch
    xl, y, z = where[0], where[1], where[3]

    def put(which, block):
        outs[0][:, which] = block.T.reshape(M, 32, N)
        emit(0, slice(None), which)

    ready(0, 1)
    signal = key_ref[...].astype(F32) * value_ref[...].astype(F32)
    put(0, signal.astype(BF16))
    ready(2)
    put(1, filt_ref[...])
    ready(3)
    put(2, query_ref[...])
    ready(6)
    for to_y in range(4):
        for to_z in range(4):
            for lo in range(2):
                first = (4 * lo + to_z) * 128
                block = d_ref[32 * to_y : 32 * to_y + 32, first : first + 128]
                for side in range(2):
                    outs[0][side * 16 + to_y * 4 + to_z, 3 + lo] = block
    emit(0, slice(None), slice(3, 5))
    ready(4)
    row = jnp.broadcast_to(skip_ref[pl.ds(xl * 4 + y, 1), :], (N, N))
    skip_s[...] = row.T.reshape(4, 32, N)
    outs[3][...] = skip_s[z]
    emit(3)
    ready(5)
    for i in range(2):
        outs[1 + i][...] = w_ref[xl ^ i]
        emit(1 + i)


def swap_quarters(blocks):
    quarter = lax.broadcasted_iota(jnp.int32, blocks[0].shape, blocks[0].ndim - 1) // 32
    axis = blocks[0].ndim - 1
    out = []
    for r in range(4):
        total = blocks[r]
        for y in range(4):
            if y != r:
                total = jnp.where(
                    quarter == y, pltpu.roll(blocks[y], (y - r) * 32 % N, axis), total
                )
        out.append(total)
    return out


def conv_kernel(_, ins, outs, scratch, ready, emit):
    in_ref, skip_ref, *tabs = ins
    conv_ref, gated_ref, sig_ref, fil_ref = outs
    ready(0)
    signal, filt, query = (in_ref[:, i].astype(F32) for i in range(3))
    ready(1, 2, 3)
    for pair in range(2):
        groups = (2 * pair, 2 * pair + 1)
        chans = slice(16 * pair, 16 * pair + 16)
        spectra = forward([rows_of(a, g) for a in (signal, filt) for g in groups], tabs)
        for i, g in enumerate(groups):
            sig_ref[g], fil_ref[g] = spectra[i], spectra[2 + i]
        emit(2, slice(2 * pair, 2 * pair + 2))
        emit(3, slice(2 * pair, 2 * pair + 2))
        conv = pair_of(*inverse([times(spectra[i], spectra[2 + i], False) for i in range(2)], tabs))
        conv = conv + skip_ref[chans, :][None] * signal[:, chans, :]
        conv = conv.astype(BF16)
        conv_ref[:, chans, :] = conv
        gated = (query[:, chans, :] * conv.astype(F32)).reshape(8, 4, 16, N)
        for y, block in enumerate(swap_quarters([gated[:, r] for r in range(4)])):
            for copy in range(4):
                gated_ref[y, copy, :, chans, :] = block.astype(BF16)
        every = slice(None)
        emit(1, every, every, every, chans)
        emit(0, every, chans)


def back_kernel(_, ins, outs, scratch, ready, emit):
    part_ref, in_ref, conv_ref, skip_ref, sig_ref, fil_ref, *tabs = ins
    (out_ref,), (gate_s,) = outs, scratch
    ready(0, 1, 2)
    for g in range(8):
        totals = []
        for y in range(4):
            total = part_ref[4 * y, g].astype(F32)
            for z in range(1, 4):
                total = total + part_ref[4 * y + z, g].astype(F32)
            totals.append(total)
        for r, grady in enumerate(swap_quarters(totals)):
            m = 4 * g + r
            out_ref[m, 0] = (grady * conv_ref[m].astype(F32)).astype(BF16)
            gate_s[m] = (grady * in_ref[m].astype(F32)).astype(BF16).astype(F32)
    emit(0, slice(None), 0)
    gate = gate_s[...]
    ready(*range(3, 8))
    spectra = forward([rows_of(gate, g) for g in range(4)], tabs)
    for which, other in ((1, fil_ref), (2, sig_ref)):
        result = inverse([times(other[g], s, True) for g, s in enumerate(spectra)], tabs)
        for pair in range(2):
            chans = slice(16 * pair, 16 * pair + 16)
            total = pair_of(*result[2 * pair : 2 * pair + 2])
            if which == 1:
                total = total + skip_ref[chans, :][None] * gate[:, chans, :]
            out_ref[:, which, chans, :] = total.astype(BF16)
        emit(0, slice(None), which)


def final_kernel(where, ins, outs, scratch, ready, emit):
    *got, key_ref, value_ref, wo_0, wo_1, wo_2, wo_3, take_ref = ins
    wo_refs, wo_ref = (wo_0, wo_1, wo_2, wo_3), outs[4]

    def get(which):
        ready(which)
        return got[which][...].reshape(M * 32, N).T

    def put(which, block):
        outs[which][...] = block.astype(BF16)
        emit(which)

    put(0, get(0))
    put(3, get(1))
    ready(*range(5, 10))
    total = wo_refs[0][...].astype(F32)
    for s in range(1, 4):
        total = total + wo_refs[s][...].astype(F32)
    wo_ref[where[0]] = total
    wo_ref[where[0] ^ 1] = take_ref[...].astype(F32)
    emit(4)
    back = get(2).astype(F32)
    ready(3, 4)
    put(1, back * value_ref[...].astype(F32))
    put(2, back * key_ref[...].astype(F32))


def grady_kernel(where, ins, outs, scratch, ready, emit):
    d_refs, w_refs, (out_ref, d_ref), (w_s,) = ins[:4], ins[4:], outs, scratch
    xl, y, q = where[0], where[1], where[2]
    for p in range(4):
        ready(p)
        for lo in range(2):
            d_ref[2 * (q ^ (2 * (p & 1) + (p >> 1))) + lo] = d_refs[p][:, lo]
    emit(1)
    for s in range(4):
        ready(4 + s)
        for i in range(2):
            w_s[(xl ^ i) * 4 + (y ^ s)] = w_refs[s][i]
    lhs = jnp.concatenate([w_s[j] for j in range(8)], axis=1)
    for g in range(0, 8, 2):
        rhs = jnp.concatenate(
            [d_ref[j, 4 * g : 4 * g + 8].reshape(2 * N, 128) for j in range(8)], axis=1
        )
        part = lax.dot_general(lhs, rhs, (((1,), (1,)), ((), ())), preferred_element_type=F32)
        part = part.astype(BF16)
        for k in range(2):
            out_ref[:, g + k] = part[:, k * N : (k + 1) * N].reshape(16, 32, N)
        emit(0, slice(None), slice(g, g + 2))


def wo_kernel(where, ins, outs, scratch, ready, emit):
    (gated_ref, d_ref), (all_s,) = ins, scratch
    ready(0, 1)
    lhs = jnp.concatenate([gated_ref[:, b].reshape(512, N) for b in range(8)], axis=1)
    for j in range(0, 8, 2):
        rhs = jnp.concatenate([d_ref[j + k].reshape(1024, 128) for k in range(2)], axis=1)
        part = dot(lhs, rhs)
        for k in range(2):
            column = j + k
            all_s[column % 4, column // 4] = part[:, k * 128 : (k + 1) * 128].astype(BF16)
    for s in range(4):
        outs[s][...] = all_s[where[1] ^ s]
        emit(s)


def give_kernel(where, ins, outs, scratch, ready, emit):
    ready(0, 1, 2, 3)
    total = ins[0][...].astype(F32)
    for s in range(1, 4):
        total = total + ins[s][...].astype(F32)
    outs[0][...] = total.astype(BF16)
    emit(0)


def index(part, xl):
    return {"xl": xl, "other": xl ^ 1}[part] if isinstance(part, str) else part


def call(kernel, ins, outs, scratch=(), parts={}, homes="", cost=2):
    n_in, n_out = len(ins), len(outs)
    in_homes, out_homes = homes[:n_in], homes[n_in:]
    assert len(out_homes) == n_out

    def whole(*refs):
        xl, y, z, xh, co = (lax.axis_index(a) for a in ("xl", "y", "z", "xh", "co"))
        where = (xl, y, 2 * xh + co, z)
        in_homes_refs, refs = list(refs[:n_in]), refs[n_in:]
        out_homes_refs, refs = refs[:n_out], refs[n_out:]
        in_copies, refs = refs[: in_homes.count("h")], refs[in_homes.count("h") :]
        out_copies, refs = list(refs[: out_homes.count("h")]), refs[out_homes.count("h") :]
        (in_sem, out_sem), rest = refs[:2], refs[2:]
        in_refs, loads, stores = [], {}, []
        for i, ref in enumerate(in_homes_refs):
            if i in parts:
                ref = ref.at[index(parts[i], xl)]
            if in_homes[i] == "h":
                copy = in_copies[len(loads)]
                loads[i] = pltpu.make_async_copy(ref, copy, in_sem.at[len(loads)])
                loads[i].start()
                ref = copy
            in_refs.append(ref)
        out_refs = [
            out_copies.pop(0) if out_homes[j] == "h" else out_homes_refs[j] for j in range(n_out)
        ]

        def ready(*which):
            for i in which:
                if i in loads:
                    loads.pop(i).wait()

        def emit(j, *index):
            if out_homes[j] == "v":
                return
            source, target = out_refs[j], out_homes_refs[j]
            if index:
                source, target = source.at[index], target.at[index]
            stores.append(pltpu.make_async_copy(source, target, out_sem.at[len(stores)]))
            stores[-1].start()

        kernel(where, in_refs, out_refs, rest, ready, emit)
        ready(*range(n_in))
        for store in stores:
            store.wait()

    shapes = [
        jax.eval_shape(lambda x, i=i: x[index(parts[i], 0)], a) if i in parts else a
        for i, a in enumerate(ins)
    ]
    buffers = [
        pltpu.VMEM(a.shape, a.dtype) for a, home in zip((*shapes, *outs), homes) if home == "h"
    ]
    spaces = {"v": pltpu.VMEM, "h": pltpu.HBM}
    specs = [pl.BlockSpec(memory_space=spaces[home]) for home in homes]
    return pl.pallas_call(
        whole,
        out_shape=[spaces[home](a.shape, a.dtype) for a, home in zip(outs, out_homes)],
        in_specs=specs[:n_in],
        out_specs=specs[n_in:],
        scratch_shapes=buffers
        + [pltpu.SemaphoreType.DMA((max(n_in, 1),)), pltpu.SemaphoreType.DMA((16,))]
        + list(scratch),
        compiler_params=PARAMS,
        cost_estimate=pl.CostEstimate(
            flops=0, bytes_accessed=cost * 3_000_000, transcendentals=0
        ),
    )(*[pltpu.with_memory_space_constraint(a, spaces[home]) for a, home in zip(ins, in_homes)])


def shape(*dims, dtype=BF16):
    return jax.ShapeDtypeStruct(dims, dtype)


CONTEXT = ("xl", "y", "z")


def flip(value, axes, sizes, by):
    total = int(np.prod(sizes))
    return lax.ppermute(value, axes, [(i, i ^ by) for i in range(total)])


def exchange(value, axes):
    return lax.all_to_all(value, axes, 0, 0)


def body(query, key_feat, value_feat, filt, skip, dout, w_out):
    tabs = tables()

    with jax.named_scope("prepare"):
        sent, keep, give, skip_c = call(
            prep_kernel,
            (key_feat, value_feat, filt, query, skip.reshape(8, 128), w_out.reshape(2, 512, 128), dout),
            [shape(M, 5, 32, N)] + [shape(512, 128)] * 2 + [shape(32, N, dtype=F32)],
            [pltpu.VMEM((4, 32, N), F32)],
            homes="hhhhhhh" + "hvvv",
            cost=3,
        )
    with jax.named_scope("to_channels"):
        held = exchange(sent, CONTEXT)
    with jax.named_scope("gather_w"):
        take = flip(give, "xl", (2,), 1)
    held, take = lax.optimization_barrier((held, take))
    with jax.named_scope("gather_d"):
        d = held[:, 3:]
        d = [d, flip(d, ("xl", "xh"), (2, 2), 3)]
    with jax.named_scope("gather_w"):
        w = jnp.stack([keep, take])
        w = [w] + [flip(w, "y", (4,), s) for s in (1, 2, 3)]
    with jax.named_scope("conv"):
        conv, gated, sig, fil = call(
            conv_kernel,
            (held, skip_c, *tabs),
            (
                shape(M, 32, N),
                shape(4, 4, 8, 32, N),
                shape(4, 256, 256, dtype=F32),
                shape(4, 256, 256, dtype=F32),
            ),
            (),
            {0: (slice(None), slice(0, 3))},
            homes="vvvv" + "hhhh",
            cost=20,
        )
    gated, w = lax.optimization_barrier((gated, w))
    with jax.named_scope("gated"):
        gated = exchange(gated.reshape(16, 8, 32, N), ("y", "z"))
    with jax.named_scope("gather_d"):
        d_pieces = d + [flip(piece, "co", (2,), 1) for piece in d]
    with jax.named_scope("grady"):
        part, d_all = call(
            grady_kernel,
            (*d_pieces, *w),
            (shape(16, 8, 32, N), shape(8, 32, 32, 128)),
            [pltpu.VMEM((8, 512, 128), BF16)],
            homes="hvvv" + "h" * 4 + "hh",
            cost=5,
        )
        part, gated = lax.optimization_barrier((part, gated))
        part = exchange(part, ("y", "z"))
    with jax.named_scope("wo"):
        wo = call(
            wo_kernel,
            (gated, d_all),
            [shape(2, 512, 128)] * 4,
            [pltpu.VMEM((4, 2, 512, 128), BF16)],
            homes="vh" + "vvvv",
            cost=5,
        )
        part, _ = lax.optimization_barrier((part, wo))
        wo = [wo[0]] + [flip(wo[s], "y", (4,), s) for s in (1, 2, 3)]
    with jax.named_scope("back"):
        (sent,) = call(
            back_kernel,
            (part, held, conv, skip_c, sig, fil, *tabs),
            [shape(M, 3, 32, N)],
            [pltpu.VMEM((M, 32, N), F32)],
            {1: (slice(None), 2)},
            homes="hhhhhhvv" + "h",
            cost=7,
        )
    with jax.named_scope("wo"):
        sent, wo = lax.optimization_barrier((sent, wo))
        (give,) = call(
            give_kernel, wo, [shape(512, 128)], (), {i: "other" for i in range(4)}, "vvvvv"
        )
        sent, give = lax.optimization_barrier((sent, give))
        take = flip(give, "xl", (2,), 1)
    with jax.named_scope("back"):
        got = exchange(sent, CONTEXT)
    with jax.named_scope("final"):
        *grads, wo_grad = call(
            final_kernel,
            (got, got, got, key_feat, value_feat, *wo, take),
            [shape(128, 1024)] * 4 + [shape(2, 512, 128, dtype=F32)],
            (),
            {0: (slice(None), 0), 1: (slice(None), 2), 2: (slice(None), 1)}
            | {i: "xl" for i in range(5, 9)},
            "vvv" + "h" * 7 + "h" * 5,
        )
    return (*grads, wo_grad.reshape(1024, 128))


def solution(mesh):
    fine = Mesh(mesh.devices.reshape(2, 4, 4, 2, 2), ("xl", "y", "z", "xh", "co"))
    tokens, channels = P(CONTEXT, ("xh", "co")), P(("xh", "co"))
    rows = P(("xh", "co"), CONTEXT)
    return jax.shard_map(
        body,
        mesh=fine,
        in_specs=(tokens, tokens, tokens, tokens, channels, tokens, rows),
        out_specs=(tokens, tokens, tokens, tokens, rows),
        check_vma=False,
    )
```

```python
import functools

import jax
import jax.numpy as jnp
import numpy as np
from jax import lax
from jax.experimental import pallas as pl
from jax.experimental.pallas import tpu as pltpu
from jax.sharding import Mesh
from jax.sharding import PartitionSpec as P

BF16 = jnp.bfloat16
F32 = jnp.float32
PARAMS = pltpu.CompilerParams(vmem_limit_bytes=16 * 1024 * 1024)

M, N = 32, 128
GROUP = 8


def split(values):
    high = values.astype(jnp.bfloat16)
    return high, (values - high.astype(values.dtype)).astype(jnp.bfloat16)


@functools.cache
def tables():
    k1, m, n = np.arange(M) + 0.25, np.arange(M), np.arange(N)
    first = 2 * np.pi * np.outer(k1, m) / M
    second = 2 * np.pi * np.outer(n, n) / N
    turn = 2 * np.pi * np.outer(k1, n) / (M * N)
    eye = np.eye(GROUP)
    one = np.kron(np.concatenate([np.cos(first), -np.sin(first)]), eye)
    cos, sin = np.cos(second), np.sin(second)
    two = np.block([[cos, -sin], [sin, cos]])
    back_two = np.block([[cos, sin], [-sin, cos]])
    back_one = one.T / (M * N)

    parts = []
    for table in (one, two, back_two, back_one[:, :256], back_one[:, 256:]):
        high = table.astype(jnp.bfloat16)
        parts += [high, (table - high.astype(np.float64)).astype(jnp.bfloat16)]
    return np.concatenate(parts), np.stack([np.cos(turn), np.sin(turn)]).astype(np.float32)


ROWS = {}
for _name, _count in (("one", 512), ("two", 256), ("back_two", 256), ("left", 256), ("right", 256)):
    for _part in "hl":
        ROWS[_name, _part] = (sum(n for _, n in ROWS.values()), _count)


def table(tabs, name):
    return [tabs[0][start : start + count] for start, count in (ROWS[name, p] for p in "hl")]


def turns(tabs):
    return [
        jnp.broadcast_to(tabs[1][i][:, None, :], (M, GROUP, N)).reshape(M * GROUP, N)
        for i in range(2)
    ]


def dot(lhs, rhs):
    return jnp.dot(lhs, rhs, preferred_element_type=F32)


def rows_of(block, group):
    part = block[:, group * GROUP : (group + 1) * GROUP, :]
    return part.reshape(M * GROUP, N).astype(BF16)


def forward(sides, tabs):
    (one_h, one_l), (two_h, two_l) = table(tabs, "one"), table(tabs, "two")
    cos, sin = turns(tabs)
    cat = jnp.concatenate(sides, axis=1)
    part = dot(one_h, cat) + dot(one_l, cat)
    half = part.shape[0] // 2
    out = []
    for index in range(len(sides)):
        lanes = slice(index * N, (index + 1) * N)
        re, im = part[:half, lanes], part[half:, lanes]
        turned = jnp.concatenate([re * cos + im * sin, im * cos - re * sin], axis=1)
        high, low = split(turned)
        out.append(dot(high, two_h) + dot(low, two_h) + dot(high, two_l))
    return out


def inverse(specs, tabs):
    two_h, two_l = table(tabs, "back_two")
    one_h, one_l = (jnp.concatenate(p, axis=1) for p in zip(table(tabs, "left"), table(tabs, "right")))
    cos, sin = turns(tabs)
    cols = []
    for spec in specs:
        high, low = split(spec)
        part = dot(high, two_h) + dot(low, two_h) + dot(high, two_l)
        re, im = part[:, :N], part[:, N:]
        cols.append(jnp.concatenate([re * cos - im * sin, im * cos + re * sin], axis=0))
    high, low = split(jnp.concatenate(cols, axis=1))
    full = dot(one_h, high) + dot(one_h, low) + dot(one_l, high)
    return [full[:, i * N : (i + 1) * N] for i in range(len(specs))]


def times(a, b, conj_a):
    are, aim, bre, bim = a[:, :N], a[:, N:], b[:, :N], b[:, N:]
    if conj_a:
        return jnp.concatenate([are * bre + aim * bim, are * bim - aim * bre], axis=1)
    return jnp.concatenate([are * bre - aim * bim, are * bim + aim * bre], axis=1)


def pair_of(first, second):
    shape = (M, GROUP, N)
    return jnp.concatenate([first.reshape(shape), second.reshape(shape)], axis=1)


def prep_kernel(where, ins, outs, scratch, ready, emit):
    key_ref, value_ref, filt_ref, query_ref, skip_ref, w_ref, d_ref = ins
    (skip_s,) = scratch
    xl, y, z = where[0], where[1], where[3]

    def put(which, block):
        outs[0][:, which] = block.T.reshape(M, 32, N).astype(BF16)
        emit(0, slice(None), which)

    ready(0, 1)
    signal = key_ref[...].astype(F32) * value_ref[...].astype(F32)
    put(0, signal.astype(BF16).astype(F32))
    ready(2)
    put(1, filt_ref[...].astype(F32))
    ready(3)
    put(2, query_ref[...].astype(F32))
    ready(6)
    for to_y in range(4):
        for to_z in range(4):
            for lo in range(2):
                first = (4 * lo + to_z) * 128
                block = d_ref[32 * to_y : 32 * to_y + 32, first : first + 128]
                for side in range(2):
                    outs[0][side * 16 + to_y * 4 + to_z, 3 + lo] = block
    emit(0, slice(None), slice(3, 5))
    ready(4)
    row = jnp.broadcast_to(skip_ref[pl.ds(xl * 4 + y, 1), :], (N, N))
    skip_s[...] = row.T.reshape(4, 32, N)
    outs[3][...] = skip_s[z]
    emit(3)
    ready(5)
    for i in range(2):
        outs[1 + i][...] = w_ref[xl ^ i]
        emit(1 + i)


def swap_quarters(blocks):
    quarter = lax.broadcasted_iota(jnp.int32, blocks[0].shape, blocks[0].ndim - 1) // 32
    axis = blocks[0].ndim - 1
    out = []
    for r in range(4):
        total = blocks[r]
        for y in range(4):
            if y != r:
                total = jnp.where(
                    quarter == y, pltpu.roll(blocks[y], (y - r) * 32 % N, axis), total
                )
        out.append(total)
    return out


def conv_kernel(_, ins, outs, scratch, ready, emit):
    in_ref, skip_ref, *tabs = ins
    conv_ref, gated_ref, sig_ref, fil_ref = outs
    ready(0)
    signal, filt, query = (in_ref[:, i].astype(F32) for i in range(3))
    ready(1, 2, 3)
    for pair in range(2):
        groups = (2 * pair, 2 * pair + 1)
        chans = slice(16 * pair, 16 * pair + 16)
        spectra = forward([rows_of(a, g) for a in (signal, filt) for g in groups], tabs)
        for i, g in enumerate(groups):
            sig_ref[g], fil_ref[g] = spectra[i], spectra[2 + i]
        emit(2, slice(2 * pair, 2 * pair + 2))
        emit(3, slice(2 * pair, 2 * pair + 2))
        conv = pair_of(*inverse([times(spectra[i], spectra[2 + i], False) for i in range(2)], tabs))
        conv = conv + skip_ref[chans, :][None] * signal[:, chans, :]
        conv = conv.astype(BF16)
        conv_ref[:, chans, :] = conv
        gated = (query[:, chans, :] * conv.astype(F32)).reshape(8, 4, 16, N)
        for y, block in enumerate(swap_quarters([gated[:, r] for r in range(4)])):
            for copy in range(4):
                gated_ref[y, copy, :, chans, :] = block.astype(BF16)
        every = slice(None)
        emit(1, every, every, every, chans)
        emit(0, every, chans)


def back_kernel(_, ins, outs, scratch, ready, emit):
    part_ref, in_ref, conv_ref, skip_ref, sig_ref, fil_ref, *tabs = ins
    (out_ref,), (gate_s,) = outs, scratch
    ready(0, 1, 2)
    for g in range(8):
        totals = []
        for y in range(4):
            total = part_ref[4 * y, g].astype(F32)
            for z in range(1, 4):
                total = total + part_ref[4 * y + z, g].astype(F32)
            totals.append(total)
        for r, grady in enumerate(swap_quarters(totals)):
            m = 4 * g + r
            out_ref[m, 0] = (grady * conv_ref[m].astype(F32)).astype(BF16)
            gate_s[m] = (grady * in_ref[m].astype(F32)).astype(BF16).astype(F32)
    emit(0, slice(None), 0)
    gate = gate_s[...]
    ready(*range(3, 8))
    for pair in range(2):
        groups = (2 * pair, 2 * pair + 1)
        chans = slice(16 * pair, 16 * pair + 16)
        spectra = forward([rows_of(gate, g) for g in groups], tabs)
        specs = [times(fil_ref[g], s, True) for g, s in zip(groups, spectra)]
        specs += [times(sig_ref[g], s, True) for g, s in zip(groups, spectra)]
        result = inverse(specs, tabs)
        back = pair_of(*result[:2]) + skip_ref[chans, :][None] * gate[:, chans, :]
        out_ref[:, 1, chans, :] = back.astype(BF16)
        emit(0, slice(None), 1, chans)
        out_ref[:, 2, chans, :] = pair_of(*result[2:]).astype(BF16)
        emit(0, slice(None), 2, chans)


def final_kernel(where, ins, outs, scratch, ready, emit):
    *got, key_ref, value_ref, wo_0, wo_1, wo_2, wo_3, take_ref = ins
    wo_refs, wo_ref = (wo_0, wo_1, wo_2, wo_3), outs[4]

    def get(which):
        ready(which)
        return got[which][...].astype(F32).reshape(M * 32, N).T

    def put(which, block):
        outs[which][...] = block.astype(BF16)
        emit(which)

    put(0, get(0))
    put(3, get(1))
    back = get(2)
    ready(3, 4)
    put(1, back * value_ref[...].astype(F32))
    put(2, back * key_ref[...].astype(F32))
    ready(*range(5, 10))
    total = wo_refs[0][...].astype(F32)
    for s in range(1, 4):
        total = total + wo_refs[s][...].astype(F32)
    wo_ref[where[0]] = total
    wo_ref[where[0] ^ 1] = take_ref[...].astype(F32)
    emit(4)


def grady_kernel(where, ins, outs, scratch, ready, emit):
    d_refs, w_refs, (out_ref, d_ref), (w_s,) = ins[:4], ins[4:], outs, scratch
    xl, y, q = where[0], where[1], where[2]
    for p in range(4):
        ready(p)
        for lo in range(2):
            d_ref[2 * (q ^ (2 * (p & 1) + (p >> 1))) + lo] = d_refs[p][:, lo]
    emit(1)
    for s in range(4):
        ready(4 + s)
        for i in range(2):
            w_s[(xl ^ i) * 4 + (y ^ s)] = w_refs[s][i]
    lhs = jnp.concatenate([w_s[j] for j in range(8)], axis=1)
    for g in range(0, 8, 2):
        rhs = jnp.concatenate(
            [d_ref[j, 4 * g : 4 * g + 8].reshape(2 * N, 128) for j in range(8)], axis=1
        )
        part = lax.dot_general(lhs, rhs, (((1,), (1,)), ((), ())), preferred_element_type=F32)
        part = part.astype(BF16)
        for k in range(2):
            out_ref[:, g + k] = part[:, k * N : (k + 1) * N].reshape(16, 32, N)
        emit(0, slice(None), slice(g, g + 2))


def wo_kernel(where, ins, outs, scratch, ready, emit):
    (gated_ref, d_ref), (all_s,) = ins, scratch
    ready(0, 1)
    lhs = jnp.concatenate([gated_ref[:, b].reshape(512, N) for b in range(8)], axis=1)
    for j in range(0, 8, 2):
        rhs = jnp.concatenate([d_ref[j + k].reshape(1024, 128) for k in range(2)], axis=1)
        part = dot(lhs, rhs)
        for k in range(2):
            column = j + k
            all_s[column % 4, column // 4] = part[:, k * 128 : (k + 1) * 128].astype(BF16)
    for s in range(4):
        outs[s][...] = all_s[where[1] ^ s]
        emit(s)


def give_kernel(where, ins, outs, scratch, ready, emit):
    ready(0, 1, 2, 3)
    total = ins[0][...].astype(F32)
    for s in range(1, 4):
        total = total + ins[s][...].astype(F32)
    outs[0][...] = total.astype(BF16)
    emit(0)


def index(part, xl):
    return {"xl": xl, "other": xl ^ 1}[part] if isinstance(part, str) else part


def call(kernel, ins, outs, scratch=(), parts={}, homes="", cost=2):
    n_in, n_out = len(ins), len(outs)
    in_homes, out_homes = homes[:n_in], homes[n_in:]
    assert len(out_homes) == n_out

    def whole(*refs):
        xl, y, z, xh, co = (lax.axis_index(a) for a in ("xl", "y", "z", "xh", "co"))
        where = (xl, y, 2 * xh + co, z)
        in_homes_refs, refs = list(refs[:n_in]), refs[n_in:]
        out_homes_refs, refs = refs[:n_out], refs[n_out:]
        in_copies, refs = refs[: in_homes.count("h")], refs[in_homes.count("h") :]
        out_copies, refs = list(refs[: out_homes.count("h")]), refs[out_homes.count("h") :]
        (in_sem, out_sem), rest = refs[:2], refs[2:]
        in_refs, loads, stores = [], {}, []
        for i, ref in enumerate(in_homes_refs):
            if i in parts:
                ref = ref.at[index(parts[i], xl)]
            if in_homes[i] == "h":
                copy = in_copies[len(loads)]
                loads[i] = pltpu.make_async_copy(ref, copy, in_sem.at[len(loads)])
                loads[i].start()
                ref = copy
            in_refs.append(ref)
        out_refs = [
            out_copies.pop(0) if out_homes[j] == "h" else out_homes_refs[j] for j in range(n_out)
        ]

        def ready(*which):
            for i in which:
                if i in loads:
                    loads.pop(i).wait()

        def emit(j, *index):
            if out_homes[j] == "v":
                return
            source, target = out_refs[j], out_homes_refs[j]
            if index:
                source, target = source.at[index], target.at[index]
            stores.append(pltpu.make_async_copy(source, target, out_sem.at[len(stores)]))
            stores[-1].start()

        kernel(where, in_refs, out_refs, rest, ready, emit)
        ready(*range(n_in))
        for store in stores:
            store.wait()

    shapes = [
        jax.eval_shape(lambda x, i=i: x[index(parts[i], 0)], a) if i in parts else a
        for i, a in enumerate(ins)
    ]
    buffers = [
        pltpu.VMEM(a.shape, a.dtype) for a, home in zip((*shapes, *outs), homes) if home == "h"
    ]
    spaces = {"v": pltpu.VMEM, "h": pltpu.HBM}
    specs = [pl.BlockSpec(memory_space=spaces[home]) for home in homes]
    return pl.pallas_call(
        whole,
        out_shape=[spaces[home](a.shape, a.dtype) for a, home in zip(outs, out_homes)],
        in_specs=specs[:n_in],
        out_specs=specs[n_in:],
        scratch_shapes=buffers
        + [pltpu.SemaphoreType.DMA((max(n_in, 1),)), pltpu.SemaphoreType.DMA((16,))]
        + list(scratch),
        compiler_params=PARAMS,
        cost_estimate=pl.CostEstimate(
            flops=0, bytes_accessed=cost * 3_000_000, transcendentals=0
        ),
    )(*[pltpu.with_memory_space_constraint(a, spaces[home]) for a, home in zip(ins, in_homes)])


def shape(*dims, dtype=BF16):
    return jax.ShapeDtypeStruct(dims, dtype)


CONTEXT = ("xl", "y", "z")


def flip(value, axes, sizes, by):
    total = int(np.prod(sizes))
    return lax.ppermute(value, axes, [(i, i ^ by) for i in range(total)])


def exchange(value, axes):
    return lax.all_to_all(value, axes, 0, 0)


def body(query, key_feat, value_feat, filt, skip, dout, w_out):
    tabs = tables()

    with jax.named_scope("prepare"):
        sent, keep, give, skip_c = call(
            prep_kernel,
            (key_feat, value_feat, filt, query, skip.reshape(8, 128), w_out.reshape(2, 512, 128), dout),
            [shape(M, 5, 32, N)] + [shape(512, 128)] * 2 + [shape(32, N, dtype=F32)],
            [pltpu.VMEM((4, 32, N), F32)],
            homes="hhhhhhh" + "hvvv",
            cost=3,
        )
    with jax.named_scope("to_channels"):
        held = exchange(sent, CONTEXT)
    with jax.named_scope("gather_w"):
        take = flip(give, "xl", (2,), 1)
    held, take = lax.optimization_barrier((held, take))
    with jax.named_scope("gather_w"):
        w = jnp.stack([keep, take])
        w = [w] + [flip(w, "y", (4,), s) for s in (1, 2, 3)]
    with jax.named_scope("conv"):
        conv, gated, sig, fil = call(
            conv_kernel,
            (held, skip_c, *tabs),
            (
                shape(M, 32, N),
                shape(4, 4, 8, 32, N),
                shape(4, 256, 256, dtype=F32),
                shape(4, 256, 256, dtype=F32),
            ),
            (),
            {0: (slice(None), slice(0, 3))},
            homes="vvvv" + "hhhh",
            cost=20,
        )
    with jax.named_scope("gather_d"):
        after, _ = lax.optimization_barrier((held, conv))
        d = after[:, 3:]
        d = [d, flip(d, ("xl", "xh"), (2, 2), 3)]
    gated, w = lax.optimization_barrier((gated, w))
    with jax.named_scope("gated"):
        gated = exchange(gated.reshape(16, 8, 32, N), ("y", "z"))
    with jax.named_scope("gather_d"):
        d_pieces = d + [flip(piece, "co", (2,), 1) for piece in d]
    with jax.named_scope("grady"):
        part, d_all = call(
            grady_kernel,
            (*d_pieces, *w),
            (shape(16, 8, 32, N), shape(8, 32, 32, 128)),
            [pltpu.VMEM((8, 512, 128), BF16)],
            homes="hvvv" + "h" * 4 + "hh",
            cost=5,
        )
        part, gated = lax.optimization_barrier((part, gated))
        part = exchange(part, ("y", "z"))
    with jax.named_scope("wo"):
        wo = call(
            wo_kernel,
            (gated, d_all),
            [shape(2, 512, 128)] * 4,
            [pltpu.VMEM((4, 2, 512, 128), BF16)],
            homes="vh" + "vvvv",
            cost=5,
        )
        part, _ = lax.optimization_barrier((part, wo))
        wo = [wo[0]] + [flip(wo[s], "y", (4,), s) for s in (1, 2, 3)]
    with jax.named_scope("back"):
        (sent,) = call(
            back_kernel,
            (part, held, conv, skip_c, sig, fil, *tabs),
            [shape(M, 3, 32, N)],
            [pltpu.VMEM((M, 32, N), F32)],
            {1: (slice(None), 2)},
            homes="hhhhhhvv" + "h",
            cost=7,
        )
    with jax.named_scope("wo"):
        sent, wo = lax.optimization_barrier((sent, wo))
        (give,) = call(
            give_kernel, wo, [shape(512, 128)], (), {i: "other" for i in range(4)}, "vvvvv"
        )
        sent, give = lax.optimization_barrier((sent, give))
        take = flip(give, "xl", (2,), 1)
    with jax.named_scope("back"):
        got = exchange(sent, CONTEXT)
    with jax.named_scope("final"):
        *grads, wo_grad = call(
            final_kernel,
            (got, got, got, key_feat, value_feat, *wo, take),
            [shape(128, 1024)] * 4 + [shape(2, 512, 128, dtype=F32)],
            (),
            {0: (slice(None), 0), 1: (slice(None), 2), 2: (slice(None), 1)}
            | {i: "xl" for i in range(5, 9)},
            "vvv" + "h" * 7 + "h" * 5,
        )
    return (*grads, wo_grad.reshape(1024, 128))


def solution(mesh):
    fine = Mesh(mesh.devices.reshape(2, 4, 4, 2, 2), ("xl", "y", "z", "xh", "co"))
    tokens, channels = P(CONTEXT, ("xh", "co")), P(("xh", "co"))
    rows = P(("xh", "co"), CONTEXT)
    return jax.shard_map(
        body,
        mesh=fine,
        in_specs=(tokens, tokens, tokens, tokens, channels, tokens, rows),
        out_specs=(tokens, tokens, tokens, tokens, rows),
        check_vma=False,
    )
```
